32 devices in a mesh: groups: 2 (over x), tm: 16 (over z, y, core).
Axes of the slice: x: 2, y: 2, z: 4, core: 2. Of those that a mesh axis runs over, the one named last changes fastest.
Arguments:
- signal: bfloat16 [128, 4096], P('groups', 'tm'), parts along dimension 0, may hold values from -6 to 6
- codes: bfloat16 [128, 128, 4096], P('groups', None, 'tm'), parts along dimension 0, may hold values from -6 to 6
- filters: float32 [128, 256], replicated, may hold values from -0.03125 to 0.03125
Outputs:
- new_codes: bfloat16 [128, 128, 4096], P('groups', None, 'tm'), parts along dimension 0
- new_filters: float32 [256, 256], P('groups'), parts along dimension 0
The draws below stay inside these ranges and needn't reach their ends.
There are 2 independent parts, one for each index of `groups`. The reference program is written for one: setup_inputs(seed, part) draws one part's arguments, and reference() takes and returns one part's arrays. A program takes and returns all parts, laid end to end along the dimension named above; an argument that names none is the same for every part. Nothing has to cross between parts.
All inputs are finite; a program needn't handle non-finite values.
Results may differ from the reference program's by a relative error of at most 0.0052.
Values may be sent and summed in bfloat16 or wider, within the bound.
No kernel may reach another device: no remote copies, remote signals or barrier semaphores. Data moves between devices by JAX's collectives and lax.ppermute only.
A program may use at most 192 MiB of HBM per device.

```python
import jax
import jax.numpy as jnp
from jax import lax

K = 128
L = 256
CH = 64
NT = 4096


def block_levels(key, shape, pieces, least, largest):
    loudness, own = 1.0, jax.random.fold_in(key, 6)
    for dim, blocks in pieces:
        steps = jnp.exp(jax.random.uniform(jax.random.fold_in(own, dim), (blocks,), jnp.float32, least / len(pieces), largest / len(pieces)))
        loudness = loudness * jnp.repeat(steps, shape[dim] // blocks).reshape([-1 if axis == dim else 1 for axis in range(len(shape))])
    return loudness


def noise(key, extent, width, reach, cuts=(), kind=jnp.bfloat16):
    values = width * jax.random.normal(key, extent, jnp.float32)
    if cuts:
        values = values * block_levels(key, extent, cuts, -0.22, 0.18)
    return jnp.clip(values, -reach, reach).astype(kind)


def setup_inputs(seed: int = 0, part: int = 0) -> dict:
    key_of = jax.random.split(jax.random.key(seed), 4)
    own_keys = jax.random.split(jax.random.fold_in(key_of[3], part), 4)
    return {
        "signal": noise(own_keys[0], (CH, NT), 1.0, 6.0, ((1, 16),)),
        "codes": noise(own_keys[1], (CH, K, NT), 1.0, 6.0, ((2, 16),)),
        "filters": noise(key_of[2], (K, L), (K * L) ** -0.5, 0.03125, (), jnp.float32),
    }


ETA_CODE = 2.0
LAM = 0.1
ETA_FILT = 0.5
EPS = 1e-06

def reference(signal, codes, filters):
    hp = lax.Precision.HIGHEST
    dims = ('NCH', 'OIH', 'NCH')
    zf = codes.astype(jnp.float32)
    dict_b = lax.optimization_barrier(filters.astype(jnp.bfloat16))
    dict_f = dict_b.astype(jnp.float32)
    recon = lax.conv_general_dilated(zf, dict_f[None, :, ::-1], (1,), [(L - 1, 0)], dimension_numbers=dims, precision=hp)[:, 0, :]
    err_b = lax.optimization_barrier((recon - signal.astype(jnp.float32)).astype(jnp.bfloat16))
    err_f = err_b.astype(jnp.float32)
    grad_codes = lax.conv_general_dilated(err_f[:, None, :], dict_f[:, None, :], (1,), [(0, L - 1)], dimension_numbers=dims, precision=hp)
    moved = zf - ETA_CODE * grad_codes
    new_codes = (moved - jnp.clip(moved, -LAM, LAM)).astype(jnp.bfloat16)
    padded = jnp.pad(err_f, ((0, 0), (0, L - 1)))[None]
    grad_dict = lax.conv_general_dilated(padded, jnp.transpose(zf, (1, 0, 2)), (1,), [(0, 0)], dimension_numbers=dims, precision=hp)[0]
    grad_dict = grad_dict / (CH * NT)
    stepped = filters - ETA_FILT * grad_dict
    new_filters = stepped / jnp.sqrt(lax.optimization_barrier(jnp.sum(stepped * stepped, axis=1, keepdims=True)) + EPS)
    return (new_codes, new_filters)
```

```python
import functools

import jax
import jax.numpy as jnp
from jax import lax
from jax.experimental import pallas as pl
from jax.experimental.pallas import tpu as pltpu
from jax.sharding import PartitionSpec as P

ETA_CODE = 2.0
LAM = 0.1
ETA_FILT = 0.5
EPS = 1e-06

F32 = jnp.float32
BF16 = jnp.bfloat16
LANES = 128
GROUP = 8
CHUNKS = 4
PACK = 16
VMEM_BYTES = 16 << 20


def chunk_starts(chans):
    return [0, chans // 8, chans // 4, chans // 2, chans]


def fetch_parts(source, target, arrived, starts):
    copies = {}
    for step, first in enumerate(starts[:-1]):
        rows = pl.ds(first, starts[step + 1] - first)
        copies[first] = pltpu.make_async_copy(source.at[rows], target.at[rows], arrived.at[step])
        copies[first].start()
    return copies


def lane_index(shape):
    return lax.broadcasted_iota(jnp.int32, shape, 1)


def parity():
    return lax.rem(lax.axis_index("tm"), 2)


def in_vmem():
    return pl.BlockSpec(memory_space=pltpu.VMEM)


def in_hbm():
    return pl.BlockSpec(memory_space=pltpu.HBM)


def spread_kernel(codes_hbm, signal_hbm, filters_hbm, near_ref, far_ref, codes_ref, signal_ref, filters_ref, shear_ref, arrived, small):
    chans, count, local_len = codes_ref.shape
    taps = filters_ref.shape[1]
    filters_in = pltpu.make_async_copy(filters_hbm, filters_ref, small.at[0])
    signal_in = pltpu.make_async_copy(signal_hbm, signal_ref, small.at[1])
    filters_in.start()
    fetches = fetch_parts(codes_hbm, codes_ref, arrived, chunk_starts(chans))
    signal_in.start()
    filters_in.wait()
    dict_t = filters_ref[...].T.astype(BF16)
    early, late = dict_t[:LANES], dict_t[LANES:]
    none = jnp.zeros((LANES, count), BF16)
    dict_rows = jnp.concatenate(
        [
            jnp.concatenate([early, none], axis=1),
            jnp.concatenate([late, early], axis=1),
            jnp.concatenate([none, late], axis=1),
        ],
        axis=0,
    )
    lane = lane_index((8, LANES))
    for c in range(0, chans, 2):
        if c in fetches:
            fetches[c].wait()
        pair = [codes_ref[c], codes_ref[c + 1]]
        halves = [jnp.concatenate([x[:, n * LANES : (n + 1) * LANES] for x in pair], axis=1) for n in range(2)]
        terms = jnp.dot(dict_rows, jnp.concatenate(halves, axis=0), preferred_element_type=F32)
        for j in range(2):
            sums = [None] * 4
            for m in range(LANES // 8):
                diagonals = [
                    terms[n * LANES + 8 * m : n * LANES + 8 * m + 8, j * LANES : (j + 1) * LANES] for n in range(3)
                ]
                if m == 0:
                    sums = diagonals + [jnp.zeros((8, LANES), F32)]
                    continue
                turned = [pltpu.roll(d, 8 * m, 1) for d in diagonals]
                inside = lane >= 8 * m
                sums[0] += jnp.where(inside, turned[0], 0.0)
                sums[1] += jnp.where(inside, turned[1], turned[0])
                sums[2] += jnp.where(inside, turned[2], turned[1])
                sums[3] += jnp.where(inside, 0.0, turned[2])
            for n in range(4):
                shear_ref[n, 8 * (c + j) : 8 * (c + j) + 8, :] = sums[n]
    total = jnp.zeros((chans, 4 * LANES), F32)
    for r in range(8):
        row = jnp.concatenate([shear_ref[n, pl.ds(r, chans, stride=8), :] for n in range(4)], axis=1)
        total += pltpu.roll(row, r, 1) if r else row
    signal_in.wait()
    own = total[:, :taps] - signal_ref[...].astype(F32)
    onward = total[:, taps:]
    even = parity() == 0
    near_ref[...] = jnp.where(even, onward, own)
    far_ref[...] = jnp.where(even, own, onward)


def hankel_block(shifted, lane):
    parts = [[], [], []]
    for m in range(LANES // PACK):
        for n in range(3):
            low = shifted[:, n * LANES : (n + 1) * LANES]
            if m:
                high = shifted[:, (n + 1) * LANES : (n + 2) * LANES]
                low = pltpu.roll(jnp.where(lane >= PACK * m, low, high), LANES - PACK * m, 1)
            parts[n].append(low)
    first, second, third = (jnp.concatenate(p, axis=0) for p in parts)
    top = jnp.concatenate([first, second], axis=1)
    bottom = jnp.concatenate([second, third], axis=1)
    return jnp.concatenate([top, bottom], axis=0)


def dict_kernel(codes_hbm, sent_near_ref, sent_far_ref, got_near_ref, got_far_ref, grad_ref, shifted_ref, codes_ref, wide_ref, arrived):
    chans, count, local_len = codes_ref.shape
    fetches = fetch_parts(codes_hbm, codes_ref, arrived, chunk_starts(chans))
    me = lax.axis_index("tm")
    even = lax.rem(me, 2) == 0
    last = me == lax.axis_size("tm") - 1
    own = jnp.where(even, sent_far_ref[...], sent_near_ref[...])
    onward = jnp.where(even, sent_near_ref[...], sent_far_ref[...])
    before = jnp.where(even, got_far_ref[...], got_near_ref[...])
    after = jnp.where(even, got_near_ref[...], got_far_ref[...])
    following = jnp.where(last, 0.0, onward + after)
    error = jnp.concatenate([own + before, following], axis=1).astype(BF16).astype(F32)
    width = error.shape[1]
    for r in range(PACK):
        moved = pltpu.roll(error, width - r, 1) if r else error
        for n in range(4):
            wide_ref[n, pl.ds(r, chans, stride=PACK), :] = moved[:, n * LANES : (n + 1) * LANES]
    lane = lane_index((PACK, LANES))

    total = jnp.zeros(grad_ref.shape, F32)
    for c in range(chans):
        if c in fetches:
            fetches[c].wait()
        rows = pl.ds(c * PACK, PACK)
        shifted = jnp.concatenate([wide_ref[n, rows, :] for n in range(4)], axis=1).astype(BF16)
        shifted_ref[c] = shifted
        total += jnp.dot(codes_ref[c], hankel_block(shifted, lane), preferred_element_type=F32)
    grad_ref[...] = total


def codes_kernel(first, after_ref, codes_hbm, shifted_ref, filters_ref, *refs):
    new_hbm, codes_ref, new_ref, arrived, left = refs[-5:]
    chans, count, local_len = codes_ref.shape
    starts = [0, chans // 4, chans]
    fetches = fetch_parts(codes_hbm.at[pl.ds(first, chans)], codes_ref, arrived, starts)
    dict_b = filters_ref[...].astype(BF16)
    lane = lane_index((PACK, LANES))
    stores = []
    done = 0
    for c in range(chans):
        grad = jnp.dot(dict_b, hankel_block(shifted_ref[first + c], lane), preferred_element_type=F32)
        if c in fetches:
            fetches[c].wait()
        moved = codes_ref[c].astype(F32) - ETA_CODE * grad
        new_ref[c] = (moved - jnp.clip(moved, -LAM, LAM)).astype(BF16)
        if c + 1 == chans or (c + 1) % GROUP == 0:
            rows = pl.ds(done, c + 1 - done)
            target = new_hbm.at[pl.ds(first + done, c + 1 - done)]
            stores.append(pltpu.make_async_copy(new_ref.at[rows], target, left.at[len(stores)]))
            stores[-1].start()
            done = c + 1
    for store in stores:
        store.wait()


def step_codes(first, chans, after, codes, shifted, filters, partial):
    count, local_len = codes.shape[1:]
    earlier = [] if partial is None else [pltpu.with_memory_space_constraint(partial, pltpu.HBM)]
    return pl.pallas_call(
        functools.partial(codes_kernel, first),
        in_specs=[in_vmem(), in_hbm(), in_vmem(), in_vmem()] + [in_hbm() for _ in earlier],
        out_specs=in_hbm(),
        out_shape=pltpu.HBM(codes.shape, BF16),
        scratch_shapes=[
            pltpu.VMEM((chans, count, local_len), BF16),
            pltpu.VMEM((chans, count, local_len), BF16),
            pltpu.SemaphoreType.DMA((2,)),
            pltpu.SemaphoreType.DMA((-(-chans // GROUP),)),
        ],
        input_output_aliases={4: 0} if earlier else {},
        compiler_params=pltpu.CompilerParams(vmem_limit_bytes=VMEM_BYTES),
        cost_estimate=pl.CostEstimate(
            flops=2 * chans * count * local_len * shifted.shape[2] // 2,
            bytes_accessed=4 * chans * count * local_len,
            transcendentals=0,
        ),
        name="codes_step",
    )(after, pltpu.with_memory_space_constraint(codes, pltpu.HBM), shifted, filters, *earlier)


def normalize_kernel(scale, new_hbm, total_ref, last_ref, filters_ref, out_ref):
    half = out_ref.shape[0]
    rows = pl.ds(pl.multiple_of(parity() * half, 8), half)
    stepped = filters_ref[rows, :] - ETA_FILT * ((total_ref[...] + last_ref[...]) / scale)
    out_ref[...] = stepped / jnp.sqrt(jnp.sum(stepped * stepped, axis=1, keepdims=True) + EPS)


def exchange(block, distance):
    size = lax.axis_size("tm")
    return lax.ppermute(block, "tm", [(i, i ^ distance) for i in range(size)])


def shards(signal, codes, filters):
    chans, count, local_len = codes.shape
    taps = filters.shape[1]
    devices = lax.axis_size("tm")
    params = pltpu.CompilerParams(vmem_limit_bytes=VMEM_BYTES)
    halo = jax.ShapeDtypeStruct((chans, taps), F32)
    matmul_flops = 2 * chans * count * local_len * taps
    sent_near, sent_far = pl.pallas_call(
        spread_kernel,
        in_specs=[in_hbm()] * 3,
        out_specs=[in_vmem()] * 2,
        out_shape=[halo, halo],
        scratch_shapes=[
            pltpu.VMEM(codes.shape, BF16),
            pltpu.VMEM(signal.shape, BF16),
            pltpu.VMEM(filters.shape, F32),
            pltpu.VMEM((4, 8 * chans, LANES), F32),
            pltpu.SemaphoreType.DMA((CHUNKS,)),
            pltpu.SemaphoreType.DMA((2,)),
        ],
        compiler_params=params,
        cost_estimate=pl.CostEstimate(flops=matmul_flops, bytes_accessed=codes.size * 2, transcendentals=0),
        name="spread",
    )(*(pltpu.with_memory_space_constraint(a, pltpu.HBM) for a in (codes, signal, filters)))

    across = [(i, i + 1) for i in range(1, devices - 1, 2)]
    across += [(j, i) for i, j in across]
    got_near = exchange(sent_near, 1)
    got_far = lax.ppermute(sent_far, "tm", across)

    terms, shifted = pl.pallas_call(
        dict_kernel,
        in_specs=[in_hbm()] + [in_vmem()] * 4,
        out_specs=[in_vmem()] * 2,
        out_shape=[
            jax.ShapeDtypeStruct((count, taps), F32),
            jax.ShapeDtypeStruct((chans, PACK, 2 * taps), BF16),
        ],
        scratch_shapes=[
            pltpu.VMEM(codes.shape, BF16),
            pltpu.VMEM((4, chans * PACK, LANES), F32),
            pltpu.SemaphoreType.DMA((CHUNKS,)),
        ],
        compiler_params=params,
        cost_estimate=pl.CostEstimate(flops=matmul_flops, bytes_accessed=codes.size * 2, transcendentals=0),
        name="dict_grad",
    )(pltpu.with_memory_space_constraint(codes, pltpu.HBM), sent_near, sent_far, got_near, got_far)

    half = count // 2
    core = parity()
    total = lax.dynamic_slice_in_dim(terms, core * half, half, 0)
    total += exchange(lax.dynamic_slice_in_dim(terms, (1 - core) * half, half, 0), 1)
    distances = [2]
    while 2 * distances[-1] < devices:
        distances.append(2 * distances[-1])
    new_codes, first = None, 0
    for place, distance in enumerate(distances):
        received = exchange(total, distance)
        end = chans * (place + 1) // len(distances)
        new_codes = step_codes(first, end - first, total, codes, shifted, filters, new_codes)
        first = end
        if distance != distances[-1]:
            total += received
    mine = pl.pallas_call(
        functools.partial(normalize_kernel, float(chans * local_len * devices)),
        in_specs=[in_hbm(), in_vmem(), in_vmem(), in_vmem()],
        out_specs=in_vmem(),
        out_shape=jax.ShapeDtypeStruct((half, taps), F32),
        compiler_params=params,
        name="normalize",
    )(pltpu.with_memory_space_constraint(new_codes, pltpu.HBM), total, received, filters)
    other = exchange(mine, 1)
    lower = core == 0
    new_filters = jnp.concatenate([jnp.where(lower, mine, other), jnp.where(lower, other, mine)], axis=0)
    return (new_codes, new_filters)


def solution(mesh):
    return jax.shard_map(
        shards,
        mesh=mesh,
        in_specs=(P("groups", "tm"), P("groups", None, "tm"), P()),
        out_specs=(P("groups", None, "tm"), P("groups", None)),
        check_vma=False,
    )
```

```python
import functools

import jax
import jax.numpy as jnp
from jax import lax
from jax.experimental import pallas as pl
from jax.experimental.pallas import tpu as pltpu
from jax.sharding import PartitionSpec as P

ETA_CODE = 2.0
LAM = 0.1
ETA_FILT = 0.5
EPS = 1e-06

F32 = jnp.float32
BF16 = jnp.bfloat16
HOP = BF16
LANES = 128
GROUP = 8
CHUNKS = 3
PACK = 16
VMEM_BYTES = 5 << 20


def chunk_starts(chans):
    return [0, chans // 8, 3 * chans // 8, chans]


def fetch_parts(source, target, arrived, starts):
    copies = {}
    for step, first in enumerate(starts[:-1]):
        rows = pl.ds(first, starts[step + 1] - first)
        copies[first] = pltpu.make_async_copy(source.at[rows], target.at[rows], arrived.at[step])
        copies[first].start()
    return copies


def lane_index(shape):
    return lax.broadcasted_iota(jnp.int32, shape, 1)


def parity():
    return lax.rem(lax.axis_index("tm"), 2)


def in_vmem():
    return pl.BlockSpec(memory_space=pltpu.VMEM)


def in_hbm():
    return pl.BlockSpec(memory_space=pltpu.HBM)


def spread_kernel(codes_hbm, signal_hbm, filters_hbm, codes_ref, near_ref, far_ref, signal_ref, filters_ref, shear_ref, arrived, small):
    chans, count, local_len = codes_ref.shape
    taps = filters_ref.shape[1]
    filters_in = pltpu.make_async_copy(filters_hbm, filters_ref, small.at[0])
    signal_in = pltpu.make_async_copy(signal_hbm, signal_ref, small.at[1])
    filters_in.start()
    fetches = fetch_parts(codes_hbm, codes_ref, arrived, chunk_starts(chans))
    signal_in.start()
    filters_in.wait()
    dict_t = filters_ref[...].T.astype(BF16)
    early, late = dict_t[:LANES], dict_t[LANES:]
    none = jnp.zeros((LANES, count), BF16)
    dict_rows = jnp.concatenate(
        [
            jnp.concatenate([early, none], axis=1),
            jnp.concatenate([late, early], axis=1),
            jnp.concatenate([none, late], axis=1),
        ],
        axis=0,
    )
    lane = lane_index((8, LANES))
    for c in range(0, chans, 2):
        if c in fetches:
            fetches[c].wait()
        pair = [codes_ref[c], codes_ref[c + 1]]
        halves = [jnp.concatenate([x[:, n * LANES : (n + 1) * LANES] for x in pair], axis=1) for n in range(2)]
        terms = jnp.dot(dict_rows, jnp.concatenate(halves, axis=0), preferred_element_type=F32)
        for j in range(2):
            sums = [None] * 4
            for m in range(LANES // 8):
                diagonals = [
                    terms[n * LANES + 8 * m : n * LANES + 8 * m + 8, j * LANES : (j + 1) * LANES] for n in range(3)
                ]
                if m == 0:
                    sums = diagonals + [jnp.zeros((8, LANES), F32)]
                    continue
                turned = [pltpu.roll(d, 8 * m, 1) for d in diagonals]
                inside = lane >= 8 * m
                sums[0] += jnp.where(inside, turned[0], 0.0)
                sums[1] += jnp.where(inside, turned[1], turned[0])
                sums[2] += jnp.where(inside, turned[2], turned[1])
                sums[3] += jnp.where(inside, 0.0, turned[2])
            for n in range(4):
                shear_ref[n, 8 * (c + j) : 8 * (c + j) + 8, :] = sums[n]
    total = jnp.zeros((chans, 4 * LANES), F32)
    for r in range(8):
        row = jnp.concatenate([shear_ref[n, pl.ds(r, chans, stride=8), :] for n in range(4)], axis=1)
        total += pltpu.roll(row, r, 1) if r else row
    signal_in.wait()
    own = total[:, :taps] - signal_ref[...].astype(F32)
    onward = total[:, taps:]
    even = parity() == 0
    near_ref[...] = jnp.where(even, onward, own)
    far_ref[...] = jnp.where(even, own, onward)


def hankel_block(shifted, lane):
    parts = [[], [], []]
    for m in range(LANES // PACK):
        for n in range(3):
            low = shifted[:, n * LANES : (n + 1) * LANES]
            if m:
                high = shifted[:, (n + 1) * LANES : (n + 2) * LANES]
                low = pltpu.roll(jnp.where(lane >= PACK * m, low, high), LANES - PACK * m, 1)
            parts[n].append(low)
    first, second, third = (jnp.concatenate(p, axis=0) for p in parts)
    top = jnp.concatenate([first, second], axis=1)
    bottom = jnp.concatenate([second, third], axis=1)
    return jnp.concatenate([top, bottom], axis=0)


def dict_kernel(codes_ref, sent_near_ref, sent_far_ref, got_near_ref, got_far_ref, mine_ref, other_ref, shifted_ref, wide_ref):
    chans, count, local_len = codes_ref.shape
    me = lax.axis_index("tm")
    even = lax.rem(me, 2) == 0
    last = me == lax.axis_size("tm") - 1
    own = jnp.where(even, sent_far_ref[...], sent_near_ref[...])
    onward = jnp.where(even, sent_near_ref[...], sent_far_ref[...])
    before = jnp.where(even, got_far_ref[...], got_near_ref[...])
    after = jnp.where(even, got_near_ref[...], got_far_ref[...])
    following = jnp.where(last, 0.0, onward + after)
    error = jnp.concatenate([own + before, following], axis=1).astype(BF16).astype(F32)
    width = error.shape[1]
    for r in range(PACK):
        moved = pltpu.roll(error, width - r, 1) if r else error
        for n in range(4):
            wide_ref[n, pl.ds(r, chans, stride=PACK), :] = moved[:, n * LANES : (n + 1) * LANES]
    lane = lane_index((PACK, LANES))

    total = jnp.zeros((count, error.shape[1] // 2), F32)
    for c in range(chans):
        rows = pl.ds(c * PACK, PACK)
        shifted = jnp.concatenate([wide_ref[n, rows, :] for n in range(4)], axis=1).astype(BF16)
        shifted_ref[c] = shifted
        total += jnp.dot(codes_ref[c], hankel_block(shifted, lane), preferred_element_type=F32)
    half = count // 2
    mine_ref[...] = jnp.where(even, total[:half], total[half:])
    other_ref[...] = jnp.where(even, total[half:], total[:half])


def codes_kernel(first, sum_ref, codes_ref, shifted_ref, filters_ref, *refs):
    new_hbm, kept_ref, new_ref, left = refs[-4:]
    kept_ref[...] = sum_ref[...]
    chans = new_ref.shape[0]
    dict_b = filters_ref[...].astype(BF16)
    lane = lane_index((PACK, LANES))
    stores = []
    done = 0
    for c in range(chans):
        grad = jnp.dot(dict_b, hankel_block(shifted_ref[first + c], lane), preferred_element_type=F32)
        moved = codes_ref[first + c].astype(F32) - ETA_CODE * grad
        new_ref[c] = (moved - jnp.clip(moved, -LAM, LAM)).astype(BF16)
        if c + 1 == chans or (c + 1) % GROUP == 0:
            rows = pl.ds(done, c + 1 - done)
            target = new_hbm.at[pl.ds(first + done, c + 1 - done)]
            stores.append(pltpu.make_async_copy(new_ref.at[rows], target, left.at[len(stores)]))
            stores[-1].start()
            done = c + 1
    for store in stores:
        store.wait()


def step_codes(first, chans, total, codes, shifted, filters, partial):
    count, local_len = codes.shape[1:]
    earlier = [] if partial is None else [pltpu.with_memory_space_constraint(partial, pltpu.HBM)]
    return pl.pallas_call(
        functools.partial(codes_kernel, first),
        in_specs=[in_vmem()] * 4 + [in_hbm() for _ in earlier],
        out_specs=[in_hbm(), in_vmem()],
        out_shape=[
            pltpu.HBM(codes.shape, BF16),
            jax.ShapeDtypeStruct(total.shape, total.dtype),
        ],
        scratch_shapes=[
            pltpu.VMEM((chans, count, local_len), BF16),
            pltpu.SemaphoreType.DMA((-(-chans // GROUP),)),
        ],
        input_output_aliases={4: 0} if earlier else {},
        compiler_params=pltpu.CompilerParams(vmem_limit_bytes=VMEM_BYTES),
        cost_estimate=pl.CostEstimate(
            flops=2 * chans * count * local_len * shifted.shape[2] // 2,
            bytes_accessed=4 * chans * count * local_len,
            transcendentals=0,
        ),
        name="codes_step",
    )(total, codes, shifted, filters, *earlier)


def normalize_kernel(scale, total_ref, last_ref, filters_ref, out_ref):
    half = out_ref.shape[0]
    rows = pl.ds(pl.multiple_of(parity() * half, 8), half)
    total = total_ref[...].astype(F32) + last_ref[...].astype(F32)
    stepped = filters_ref[rows, :] - ETA_FILT * (total / scale)
    out_ref[...] = stepped / jnp.sqrt(jnp.sum(stepped * stepped, axis=1, keepdims=True) + EPS)


def join_kernel(mine_ref, other_ref, out_ref):
    half = mine_ref.shape[0]
    even = parity() == 0
    out_ref[:half, :] = jnp.where(even, mine_ref[...], other_ref[...])
    out_ref[half:, :] = jnp.where(even, other_ref[...], mine_ref[...])


def exchange(block, distance):
    size = lax.axis_size("tm")
    return lax.ppermute(block, "tm", [(i, i ^ distance) for i in range(size)])


def shards(signal, codes, filters):
    chans, count, local_len = codes.shape
    taps = filters.shape[1]
    devices = lax.axis_size("tm")
    half = count // 2
    params = pltpu.CompilerParams(vmem_limit_bytes=VMEM_BYTES)
    halo = jax.ShapeDtypeStruct((chans, taps), F32)
    matmul_flops = 2 * chans * count * local_len * taps
    held, sent_near, sent_far = pl.pallas_call(
        spread_kernel,
        in_specs=[in_hbm()] * 3,
        out_specs=[in_vmem()] * 3,
        out_shape=[jax.ShapeDtypeStruct(codes.shape, BF16), halo, halo],
        scratch_shapes=[
            pltpu.VMEM(signal.shape, BF16),
            pltpu.VMEM(filters.shape, F32),
            pltpu.VMEM((4, 8 * chans, LANES), F32),
            pltpu.SemaphoreType.DMA((CHUNKS,)),
            pltpu.SemaphoreType.DMA((2,)),
        ],
        compiler_params=params,
        cost_estimate=pl.CostEstimate(flops=matmul_flops, bytes_accessed=codes.size * 2, transcendentals=0),
        name="spread",
    )(*(pltpu.with_memory_space_constraint(a, pltpu.HBM) for a in (codes, signal, filters)))

    across = [(i, i + 1) for i in range(1, devices - 1, 2)]
    across += [(j, i) for i, j in across]
    got_near = exchange(sent_near, 1)
    got_far = lax.ppermute(sent_far, "tm", across)

    mine, other, shifted = pl.pallas_call(
        dict_kernel,
        in_specs=[in_vmem()] * 5,
        out_specs=[in_vmem()] * 3,
        out_shape=[
            jax.ShapeDtypeStruct((half, taps), F32),
            jax.ShapeDtypeStruct((half, taps), F32),
            jax.ShapeDtypeStruct((chans, PACK, 2 * taps), BF16),
        ],
        scratch_shapes=[pltpu.VMEM((4, chans * PACK, LANES), F32)],
        compiler_params=params,
        cost_estimate=pl.CostEstimate(flops=matmul_flops, bytes_accessed=codes.size * 2, transcendentals=0),
        name="dict_grad",
    )(held, sent_near, sent_far, got_near, got_far)

    total = mine + exchange(other, 1)
    distances = [2]
    while 2 * distances[-1] < devices:
        distances.append(2 * distances[-1])
    new_codes, first = None, 0
    for place, distance in enumerate(distances):
        sent = total.astype(HOP)
        received = exchange(sent, distance)
        end = chans * (place + 1) // len(distances)
        new_codes, kept = step_codes(first, end - first, sent, held, shifted, filters, new_codes)
        first = end
        total = kept.astype(F32) + received.astype(F32)
    mine = pl.pallas_call(
        functools.partial(normalize_kernel, float(chans * local_len * devices)),
        in_specs=[in_vmem()] * 3,
        out_specs=in_vmem(),
        out_shape=jax.ShapeDtypeStruct((half, taps), F32),
        compiler_params=params,
        name="normalize",
    )(kept, received, filters)
    new_filters = pl.pallas_call(
        join_kernel,
        in_specs=[in_vmem()] * 2,
        out_specs=in_vmem(),
        out_shape=jax.ShapeDtypeStruct((count, taps), F32),
        compiler_params=params,
        name="join",
    )(mine, exchange(mine, 1))
    return (new_codes, new_filters)


def solution(mesh):
    return jax.shard_map(
        shards,
        mesh=mesh,
        in_specs=(P("groups", "tm"), P("groups", None, "tm"), P()),
        out_specs=(P("groups", None, "tm"), P("groups", None)),
        check_vma=False,
    )
```

```python
import functools

import jax
import jax.numpy as jnp
from jax import lax
from jax.experimental import pallas as pl
from jax.experimental.pallas import tpu as pltpu
from jax.sharding import PartitionSpec as P

ETA_CODE = 2.0
LAM = 0.1
ETA_FILT = 0.5
EPS = 1e-06

F32 = jnp.float32
BF16 = jnp.bfloat16
HOP = BF16
LANES = 128
GROUP = 8
CHUNKS = 3
PACK = 16
VMEM_BYTES = 5 << 20


def chunk_starts(chans):
    return [0, chans // 8, 3 * chans // 8, chans]


def fetch_parts(source, target, arrived, starts):
    copies = {}
    for step, first in enumerate(starts[:-1]):
        rows = pl.ds(first, starts[step + 1] - first)
        copies[first] = pltpu.make_async_copy(source.at[rows], target.at[rows], arrived.at[step])
        copies[first].start()
    return copies


def lane_index(shape):
    return lax.broadcasted_iota(jnp.int32, shape, 1)


def parity():
    return lax.rem(lax.axis_index("tm"), 2)


def in_vmem():
    return pl.BlockSpec(memory_space=pltpu.VMEM)


def in_hbm():
    return pl.BlockSpec(memory_space=pltpu.HBM)


def spread_kernel(codes_hbm, signal_hbm, filters_hbm, codes_ref, near_ref, far_ref, signal_ref, filters_ref, shear_ref, arrived, small):
    chans, count, local_len = codes_ref.shape
    taps = filters_ref.shape[1]
    filters_in = pltpu.make_async_copy(filters_hbm, filters_ref, small.at[0])
    signal_in = pltpu.make_async_copy(signal_hbm, signal_ref, small.at[1])
    filters_in.start()
    fetches = fetch_parts(codes_hbm, codes_ref, arrived, chunk_starts(chans))
    signal_in.start()
    filters_in.wait()
    dict_t = filters_ref[...].T.astype(BF16)
    early, late = dict_t[:LANES], dict_t[LANES:]
    none = jnp.zeros((LANES, count), BF16)
    dict_rows = jnp.concatenate(
        [
            jnp.concatenate([early, none], axis=1),
            jnp.concatenate([late, early], axis=1),
            jnp.concatenate([none, late], axis=1),
        ],
        axis=0,
    )
    lane = lane_index((8, LANES))
    for c in range(0, chans, 2):
        if c in fetches:
            fetches[c].wait()
        pair = [codes_ref[c], codes_ref[c + 1]]
        halves = [jnp.concatenate([x[:, n * LANES : (n + 1) * LANES] for x in pair], axis=1) for n in range(2)]
        terms = jnp.dot(dict_rows, jnp.concatenate(halves, axis=0), preferred_element_type=F32)
        for j in range(2):
            sums = [None] * 4
            for m in range(LANES // 8):
                diagonals = [
                    terms[n * LANES + 8 * m : n * LANES + 8 * m + 8, j * LANES : (j + 1) * LANES] for n in range(3)
                ]
                if m == 0:
                    sums = diagonals + [jnp.zeros((8, LANES), F32)]
                    continue
                turned = [pltpu.roll(d, 8 * m, 1) for d in diagonals]
                inside = lane >= 8 * m
                sums[0] += jnp.where(inside, turned[0], 0.0)
                sums[1] += jnp.where(inside, turned[1], turned[0])
                sums[2] += jnp.where(inside, turned[2], turned[1])
                sums[3] += jnp.where(inside, 0.0, turned[2])
            for n in range(4):
                shear_ref[n, 8 * (c + j) : 8 * (c + j) + 8, :] = sums[n]
    total = jnp.zeros((chans, 4 * LANES), F32)
    for r in range(8):
        row = jnp.concatenate([shear_ref[n, pl.ds(r, chans, stride=8), :] for n in range(4)], axis=1)
        total += pltpu.roll(row, r, 1) if r else row
    signal_in.wait()
    own = total[:, :taps] - signal_ref[...].astype(F32)
    onward = total[:, taps:]
    even = parity() == 0
    near_ref[...] = jnp.where(even, onward, own)
    far_ref[...] = jnp.where(even, own, onward)


def hankel_block(shifted, lane):
    parts = [[], [], []]
    for m in range(LANES // PACK):
        for n in range(3):
            low = shifted[:, n * LANES : (n + 1) * LANES]
            if m:
                high = shifted[:, (n + 1) * LANES : (n + 2) * LANES]
                low = pltpu.roll(jnp.where(lane >= PACK * m, low, high), LANES - PACK * m, 1)
            parts[n].append(low)
    first, second, third = (jnp.concatenate(p, axis=0) for p in parts)
    top = jnp.concatenate([first, second], axis=1)
    bottom = jnp.concatenate([second, third], axis=1)
    return jnp.concatenate([top, bottom], axis=0)


def dict_kernel(codes_ref, sent_near_ref, sent_far_ref, got_near_ref, got_far_ref, mine_ref, other_ref, shifted_ref, wide_ref):
    chans, count, local_len = codes_ref.shape
    me = lax.axis_index("tm")
    even = lax.rem(me, 2) == 0
    last = me == lax.axis_size("tm") - 1
    own = jnp.where(even, sent_far_ref[...], sent_near_ref[...])
    onward = jnp.where(even, sent_near_ref[...], sent_far_ref[...])
    before = jnp.where(even, got_far_ref[...], got_near_ref[...])
    after = jnp.where(even, got_near_ref[...], got_far_ref[...])
    following = jnp.where(last, 0.0, onward + after)
    error = jnp.concatenate([own + before, following], axis=1).astype(BF16).astype(F32)
    width = error.shape[1]
    for r in range(PACK):
        moved = pltpu.roll(error, width - r, 1) if r else error
        for n in range(4):
            wide_ref[n, pl.ds(r, chans, stride=PACK), :] = moved[:, n * LANES : (n + 1) * LANES]
    lane = lane_index((PACK, LANES))

    total = jnp.zeros((count, error.shape[1] // 2), F32)
    for c in range(chans):
        rows = pl.ds(c * PACK, PACK)
        shifted = jnp.concatenate([wide_ref[n, rows, :] for n in range(4)], axis=1).astype(BF16)
        shifted_ref[c] = shifted
        total += jnp.dot(codes_ref[c], hankel_block(shifted, lane), preferred_element_type=F32)
    half = count // 2
    mine_ref[...] = jnp.where(even, total[:half], total[half:])
    other_ref[...] = jnp.where(even, total[half:], total[:half])


def codes_kernel(first, sum_ref, codes_ref, shifted_ref, filters_ref, *refs):
    new_hbm, kept_ref, new_ref, left = refs[-4:]
    kept_ref[...] = sum_ref[...]
    chans = new_ref.shape[0]
    dict_b = filters_ref[...].astype(BF16)
    lane = lane_index((PACK, LANES))
    stores = []
    done = 0
    for c in range(chans):
        grad = jnp.dot(dict_b, hankel_block(shifted_ref[first + c], lane), preferred_element_type=F32)
        moved = codes_ref[first + c].astype(F32) - ETA_CODE * grad
        new_ref[c] = (moved - jnp.clip(moved, -LAM, LAM)).astype(BF16)
        if c + 1 == chans or (c + 1) % GROUP == 0:
            rows = pl.ds(done, c + 1 - done)
            target = new_hbm.at[pl.ds(first + done, c + 1 - done)]
            stores.append(pltpu.make_async_copy(new_ref.at[rows], target, left.at[len(stores)]))
            stores[-1].start()
            done = c + 1
    for store in stores:
        store.wait()


def step_codes(first, chans, total, codes, shifted, filters, partial):
    count, local_len = codes.shape[1:]
    earlier = [] if partial is None else [pltpu.with_memory_space_constraint(partial, pltpu.HBM)]
    return pl.pallas_call(
        functools.partial(codes_kernel, first),
        in_specs=[in_vmem()] * 4 + [in_hbm() for _ in earlier],
        out_specs=[in_hbm(), in_vmem()],
        out_shape=[
            pltpu.HBM(codes.shape, BF16),
            jax.ShapeDtypeStruct(total.shape, total.dtype),
        ],
        scratch_shapes=[
            pltpu.VMEM((chans, count, local_len), BF16),
            pltpu.SemaphoreType.DMA((-(-chans // GROUP),)),
        ],
        input_output_aliases={4: 0} if earlier else {},
        compiler_params=pltpu.CompilerParams(vmem_limit_bytes=VMEM_BYTES),
        cost_estimate=pl.CostEstimate(
            flops=2 * chans * count * local_len * shifted.shape[2] // 2,
            bytes_accessed=4 * chans * count * local_len,
            transcendentals=0,
        ),
        name="codes_step",
    )(total, codes, shifted, filters, *earlier)


def normalize_kernel(scale, total_ref, last_ref, filters_ref, out_ref):
    half = out_ref.shape[0]
    rows = pl.ds(pl.multiple_of(parity() * half, 8), half)
    total = total_ref[...].astype(F32) + last_ref[...].astype(F32)
    stepped = filters_ref[rows, :] - ETA_FILT * (total / scale)
    out_ref[...] = stepped / jnp.sqrt(jnp.sum(stepped * stepped, axis=1, keepdims=True) + EPS)


def join_kernel(mine_ref, other_ref, out_ref):
    half = mine_ref.shape[0]
    even = parity() == 0
    out_ref[:half, :] = jnp.where(even, mine_ref[...], other_ref[...])
    out_ref[half:, :] = jnp.where(even, other_ref[...], mine_ref[...])


def exchange_rounds(devices):
    distance, rounds = 2, []
    while distance < devices:
        both = 4 * distance < devices
        rounds.append([distance, 2 * distance, 3 * distance] if both else [distance])
        distance *= 4 if both else 2
    return rounds


def part_ends(chans, rounds):
    weights = [4 if len(distances) > 1 else 3 for distances in rounds]
    return [chans * sum(weights[:n]) // sum(weights) for n in range(len(rounds) + 1)]


def exchange(block, distance):
    size = lax.axis_size("tm")
    return lax.ppermute(block, "tm", [(i, i ^ distance) for i in range(size)])


def shards(signal, codes, filters):
    chans, count, local_len = codes.shape
    taps = filters.shape[1]
    devices = lax.axis_size("tm")
    half = count // 2
    params = pltpu.CompilerParams(vmem_limit_bytes=VMEM_BYTES)
    halo = jax.ShapeDtypeStruct((chans, taps), F32)
    matmul_flops = 2 * chans * count * local_len * taps
    held, sent_near, sent_far = pl.pallas_call(
        spread_kernel,
        in_specs=[in_hbm()] * 3,
        out_specs=[in_vmem()] * 3,
        out_shape=[jax.ShapeDtypeStruct(codes.shape, BF16), halo, halo],
        scratch_shapes=[
            pltpu.VMEM(signal.shape, BF16),
            pltpu.VMEM(filters.shape, F32),
            pltpu.VMEM((4, 8 * chans, LANES), F32),
            pltpu.SemaphoreType.DMA((CHUNKS,)),
            pltpu.SemaphoreType.DMA((2,)),
        ],
        compiler_params=params,
        cost_estimate=pl.CostEstimate(flops=matmul_flops, bytes_accessed=codes.size * 2, transcendentals=0),
        name="spread",
    )(*(pltpu.with_memory_space_constraint(a, pltpu.HBM) for a in (codes, signal, filters)))

    across = [(i, i + 1) for i in range(1, devices - 1, 2)]
    across += [(j, i) for i, j in across]
    got_far = lax.ppermute(sent_far, "tm", across)
    got_near = exchange(sent_near, 1)

    mine, other, shifted = pl.pallas_call(
        dict_kernel,
        in_specs=[in_vmem()] * 5,
        out_specs=[in_vmem()] * 3,
        out_shape=[
            jax.ShapeDtypeStruct((half, taps), F32),
            jax.ShapeDtypeStruct((half, taps), F32),
            jax.ShapeDtypeStruct((chans, PACK, 2 * taps), BF16),
        ],
        scratch_shapes=[pltpu.VMEM((4, chans * PACK, LANES), F32)],
        compiler_params=params,
        cost_estimate=pl.CostEstimate(flops=matmul_flops, bytes_accessed=codes.size * 2, transcendentals=0),
        name="dict_grad",
    )(held, sent_near, sent_far, got_near, got_far)

    total = mine + exchange(other, 1)
    rounds = exchange_rounds(devices)
    ends = part_ends(chans, rounds)
    new_codes = None
    for place, distances in enumerate(rounds):
        sent = total.astype(HOP)
        received = [exchange(sent, d) for d in distances]
        first, end = ends[place], ends[place + 1]
        new_codes, kept = step_codes(first, end - first, sent, held, shifted, filters, new_codes)
        if place + 1 < len(rounds):
            total = kept.astype(F32) + received[0].astype(F32)
            if len(received) > 1:
                total += received[1].astype(F32) + received[2].astype(F32)
    mine = pl.pallas_call(
        functools.partial(normalize_kernel, float(chans * local_len * devices)),
        in_specs=[in_vmem()] * 3,
        out_specs=in_vmem(),
        out_shape=jax.ShapeDtypeStruct((half, taps), F32),
        compiler_params=params,
        name="normalize",
    )(kept, received[0], filters)
    new_filters = pl.pallas_call(
        join_kernel,
        in_specs=[in_vmem()] * 2,
        out_specs=in_vmem(),
        out_shape=jax.ShapeDtypeStruct((count, taps), F32),
        compiler_params=params,
        name="join",
    )(mine, exchange(mine, 1))
    return (new_codes, new_filters)


def solution(mesh):
    return jax.shard_map(
        shards,
        mesh=mesh,
        in_specs=(P("groups", "tm"), P("groups", None, "tm"), P()),
        out_specs=(P("groups", None, "tm"), P("groups", None)),
        check_vma=False,
    )
```

```python
import functools

import jax
import jax.numpy as jnp
from jax import lax
from jax.experimental import pallas as pl
from jax.experimental.pallas import tpu as pltpu
from jax.sharding import PartitionSpec as P

ETA_CODE = 2.0
LAM = 0.1
ETA_FILT = 0.5
EPS = 1e-06

F32 = jnp.float32
BF16 = jnp.bfloat16
HOP = BF16
LANES = 128
GROUP = 8
CHUNKS = 3
PACK = 16
VMEM_BYTES = 5 << 20


def chunk_starts(chans):
    return [0, chans // 8, 3 * chans // 8, chans]


def fetch_parts(source, target, arrived, starts):
    copies = {}
    for step, first in enumerate(starts[:-1]):
        rows = pl.ds(first, starts[step + 1] - first)
        copies[first] = pltpu.make_async_copy(source.at[rows], target.at[rows], arrived.at[step])
        copies[first].start()
    return copies


def lane_index(shape):
    return lax.broadcasted_iota(jnp.int32, shape, 1)


def parity():
    return lax.rem(lax.axis_index("tm"), 2)


def in_vmem():
    return pl.BlockSpec(memory_space=pltpu.VMEM)


def in_hbm():
    return pl.BlockSpec(memory_space=pltpu.HBM)


def spread_kernel(codes_hbm, signal_hbm, filters_hbm, codes_ref, filters_ref, far_ref, far_sent_ref, near_ref, signal_ref, shear_ref, arrived, small):
    chans, count, local_len = codes_ref.shape
    taps = filters_ref.shape[1]
    filters_in = pltpu.make_async_copy(filters_hbm, filters_ref, small.at[0])
    signal_in = pltpu.make_async_copy(signal_hbm, signal_ref, small.at[1])
    filters_in.start()
    fetches = fetch_parts(codes_hbm, codes_ref, arrived, chunk_starts(chans))
    signal_in.start()
    filters_in.wait()
    dict_t = filters_ref[...].T.astype(BF16)
    early, late = dict_t[:LANES], dict_t[LANES:]
    none = jnp.zeros((LANES, count), BF16)
    dict_rows = jnp.concatenate(
        [
            jnp.concatenate([early, none], axis=1),
            jnp.concatenate([late, early], axis=1),
            jnp.concatenate([none, late], axis=1),
        ],
        axis=0,
    )
    lane = lane_index((8, LANES))
    for c in range(0, chans, 2):
        if c in fetches:
            fetches[c].wait()
        pair = [codes_ref[c], codes_ref[c + 1]]
        halves = [jnp.concatenate([x[:, n * LANES : (n + 1) * LANES] for x in pair], axis=1) for n in range(2)]
        terms = jnp.dot(dict_rows, jnp.concatenate(halves, axis=0), preferred_element_type=F32)
        for j in range(2):
            sums = [None] * 4
            for m in range(LANES // 8):
                diagonals = [
                    terms[n * LANES + 8 * m : n * LANES + 8 * m + 8, j * LANES : (j + 1) * LANES] for n in range(3)
                ]
                if m == 0:
                    sums = diagonals + [jnp.zeros((8, LANES), F32)]
                    continue
                turned = [pltpu.roll(d, 8 * m, 1) for d in diagonals]
                inside = lane >= 8 * m
                sums[0] += jnp.where(inside, turned[0], 0.0)
                sums[1] += jnp.where(inside, turned[1], turned[0])
                sums[2] += jnp.where(inside, turned[2], turned[1])
                sums[3] += jnp.where(inside, 0.0, turned[2])
            for n in range(4):
                shear_ref[n, 8 * (c + j) : 8 * (c + j) + 8, :] = sums[n]
    total = jnp.zeros((chans, 4 * LANES), F32)
    for r in range(8):
        row = jnp.concatenate([shear_ref[n, pl.ds(r, chans, stride=8), :] for n in range(4)], axis=1)
        total += pltpu.roll(row, r, 1) if r else row
    signal_in.wait()
    own = total[:, :taps] - signal_ref[...].astype(F32)
    onward = total[:, taps:]
    even = parity() == 0
    near_ref[...] = jnp.where(even, onward, own)
    far = jnp.where(even, own, onward)
    far_ref[...] = far
    far_sent_ref[...] = far.astype(far_sent_ref.dtype)


def hankel_block(shifted, lane):
    parts = [[], [], []]
    for m in range(LANES // PACK):
        for n in range(3):
            low = shifted[:, n * LANES : (n + 1) * LANES]
            if m:
                high = shifted[:, (n + 1) * LANES : (n + 2) * LANES]
                low = pltpu.roll(jnp.where(lane >= PACK * m, low, high), LANES - PACK * m, 1)
            parts[n].append(low)
    first, second, third = (jnp.concatenate(p, axis=0) for p in parts)
    top = jnp.concatenate([first, second], axis=1)
    bottom = jnp.concatenate([second, third], axis=1)
    return jnp.concatenate([top, bottom], axis=0)


def dict_kernel(codes_ref, sent_near_ref, sent_far_ref, got_near_ref, got_far_ref, mine_ref, other_ref, shifted_ref, wide_ref):
    chans, count, local_len = codes_ref.shape
    me = lax.axis_index("tm")
    even = lax.rem(me, 2) == 0
    last = me == lax.axis_size("tm") - 1
    own = jnp.where(even, sent_far_ref[...], sent_near_ref[...])
    onward = jnp.where(even, sent_near_ref[...], sent_far_ref[...])
    got_far = got_far_ref[...].astype(F32)
    before = jnp.where(even, got_far, got_near_ref[...])
    after = jnp.where(even, got_near_ref[...], got_far)
    following = jnp.where(last, 0.0, onward + after)
    error = jnp.concatenate([own + before, following], axis=1).astype(BF16)
    width = error.shape[1]
    lane = lane_index((PACK, LANES))
    total = jnp.zeros((count, width // 2), F32)
    for first in range(0, chans, PACK):
        rows = error[first : first + PACK]
        for r in range(PACK):
            moved = (pltpu.roll(rows, width - r, 1) if r else rows).astype(F32)
            for n in range(4):
                wide_ref[n, pl.ds(first * PACK + r, PACK, stride=PACK), :] = moved[:, n * LANES : (n + 1) * LANES]
        for c in range(first, first + PACK):
            rows_c = pl.ds(c * PACK, PACK)
            shifted = jnp.concatenate([wide_ref[n, rows_c, :] for n in range(4)], axis=1).astype(BF16)
            shifted_ref[c] = shifted
            total += jnp.dot(codes_ref[c], hankel_block(shifted, lane), preferred_element_type=F32)
    half = count // 2
    mine_ref[...] = jnp.where(even, total[:half], total[half:])
    other_ref[...] = jnp.where(even, total[half:], total[:half])


def codes_kernel(first, sum_ref, codes_ref, shifted_ref, filters_ref, *refs):
    new_hbm, kept_ref, new_ref, left = refs[-4:]
    kept_ref[...] = sum_ref[...]
    chans = new_ref.shape[0]
    dict_b = filters_ref[...].astype(BF16)
    lane = lane_index((PACK, LANES))
    stores = []
    done = 0
    for c in range(chans):
        grad = jnp.dot(dict_b, hankel_block(shifted_ref[first + c], lane), preferred_element_type=F32)
        moved = codes_ref[first + c].astype(F32) - ETA_CODE * grad
        new_ref[c] = (moved - jnp.clip(moved, -LAM, LAM)).astype(BF16)
        if c + 1 == chans or (c + 1) % GROUP == 0:
            rows = pl.ds(done, c + 1 - done)
            target = new_hbm.at[pl.ds(first + done, c + 1 - done)]
            stores.append(pltpu.make_async_copy(new_ref.at[rows], target, left.at[len(stores)]))
            stores[-1].start()
            done = c + 1
    for store in stores:
        store.wait()


def step_codes(first, chans, total, codes, shifted, filters, partial):
    count, local_len = codes.shape[1:]
    earlier = [] if partial is None else [pltpu.with_memory_space_constraint(partial, pltpu.HBM)]
    return pl.pallas_call(
        functools.partial(codes_kernel, first),
        in_specs=[in_vmem()] * 4 + [in_hbm() for _ in earlier],
        out_specs=[in_hbm(), in_vmem()],
        out_shape=[
            pltpu.HBM(codes.shape, BF16),
            jax.ShapeDtypeStruct(total.shape, total.dtype),
        ],
        scratch_shapes=[
            pltpu.VMEM((chans, count, local_len), BF16),
            pltpu.SemaphoreType.DMA((-(-chans // GROUP),)),
        ],
        input_output_aliases={4: 0} if earlier else {},
        compiler_params=pltpu.CompilerParams(vmem_limit_bytes=VMEM_BYTES),
        cost_estimate=pl.CostEstimate(
            flops=2 * chans * count * local_len * shifted.shape[2] // 2,
            bytes_accessed=4 * chans * count * local_len,
            transcendentals=0,
        ),
        name="codes_step",
    )(total, codes, shifted, filters, *earlier)


def normalize_kernel(scale, total_ref, last_ref, filters_ref, out_ref):
    half = out_ref.shape[0]
    rows = pl.ds(pl.multiple_of(parity() * half, 8), half)
    total = total_ref[...].astype(F32) + last_ref[...].astype(F32)
    stepped = filters_ref[rows, :] - ETA_FILT * (total / scale)
    out_ref[...] = stepped / jnp.sqrt(jnp.sum(stepped * stepped, axis=1, keepdims=True) + EPS)


def join_kernel(mine_ref, other_ref, out_ref):
    half = mine_ref.shape[0]
    even = parity() == 0
    out_ref[:half, :] = jnp.where(even, mine_ref[...], other_ref[...])
    out_ref[half:, :] = jnp.where(even, other_ref[...], mine_ref[...])


def exchange_rounds(devices):
    distance, rounds = 2, []
    while distance < devices:
        both = 4 * distance < devices
        rounds.append([distance, 2 * distance, 3 * distance] if both else [distance])
        distance *= 4 if both else 2
    return rounds


def part_ends(chans, rounds):
    weights = [4 if len(distances) > 1 else 3 for distances in rounds]
    return [chans * sum(weights[:n]) // sum(weights) for n in range(len(rounds) + 1)]


def exchange(block, distance):
    size = lax.axis_size("tm")
    return lax.ppermute(block, "tm", [(i, i ^ distance) for i in range(size)])


def shards(signal, codes, filters):
    chans, count, local_len = codes.shape
    taps = filters.shape[1]
    devices = lax.axis_size("tm")
    half = count // 2
    params = pltpu.CompilerParams(vmem_limit_bytes=VMEM_BYTES)
    halo = jax.ShapeDtypeStruct((chans, taps), F32)
    matmul_flops = 2 * chans * count * local_len * taps
    held, held_filters, far, sent_far, sent_near = pl.pallas_call(
        spread_kernel,
        in_specs=[in_hbm()] * 3,
        out_specs=[in_vmem()] * 5,
        out_shape=[
            jax.ShapeDtypeStruct(codes.shape, BF16),
            jax.ShapeDtypeStruct(filters.shape, F32),
            halo,
            jax.ShapeDtypeStruct(halo.shape, HOP),
            halo,
        ],
        scratch_shapes=[
            pltpu.VMEM(signal.shape, BF16),
            pltpu.VMEM((4, 8 * chans, LANES), F32),
            pltpu.SemaphoreType.DMA((CHUNKS,)),
            pltpu.SemaphoreType.DMA((2,)),
        ],
        compiler_params=params,
        cost_estimate=pl.CostEstimate(flops=matmul_flops, bytes_accessed=codes.size * 2, transcendentals=0),
        name="spread",
    )(*(pltpu.with_memory_space_constraint(a, pltpu.HBM) for a in (codes, signal, filters)))

    across = [(i, i + 1) for i in range(1, devices - 1, 2)]
    across += [(j, i) for i, j in across]
    got_far = lax.ppermute(sent_far, "tm", across)
    got_near = exchange(sent_near, 1)

    mine, other, shifted = pl.pallas_call(
        dict_kernel,
        in_specs=[in_vmem()] * 5,
        out_specs=[in_vmem()] * 3,
        out_shape=[
            jax.ShapeDtypeStruct((half, taps), F32),
            jax.ShapeDtypeStruct((half, taps), F32),
            jax.ShapeDtypeStruct((chans, PACK, 2 * taps), BF16),
        ],
        scratch_shapes=[pltpu.VMEM((4, chans * PACK, LANES), F32)],
        compiler_params=params,
        cost_estimate=pl.CostEstimate(flops=matmul_flops, bytes_accessed=codes.size * 2, transcendentals=0),
        name="dict_grad",
    )(held, sent_near, far, got_near, got_far)

    total = mine + exchange(other, 1)
    rounds = exchange_rounds(devices)
    ends = part_ends(chans, rounds)
    new_codes = None
    for place, distances in enumerate(rounds):
        sent = total.astype(HOP)
        received = [exchange(sent, d) for d in distances]
        first, end = ends[place], ends[place + 1]
        new_codes, kept = step_codes(first, end - first, sent, held, shifted, held_filters, new_codes)
        if place + 1 < len(rounds):
            total = kept.astype(F32) + received[0].astype(F32)
            if len(received) > 1:
                total += received[1].astype(F32) + received[2].astype(F32)
    mine = pl.pallas_call(
        functools.partial(normalize_kernel, float(chans * local_len * devices)),
        in_specs=[in_vmem()] * 3,
        out_specs=in_vmem(),
        out_shape=jax.ShapeDtypeStruct((half, taps), F32),
        compiler_params=params,
        name="normalize",
    )(kept, received[0], held_filters)
    new_filters = pl.pallas_call(
        join_kernel,
        in_specs=[in_vmem()] * 2,
        out_specs=in_vmem(),
        out_shape=jax.ShapeDtypeStruct((count, taps), F32),
        compiler_params=params,
        name="join",
    )(mine, exchange(mine, 1))
    return (new_codes, new_filters)


def solution(mesh):
    return jax.shard_map(
        shards,
        mesh=mesh,
        in_specs=(P("groups", "tm"), P("groups", None, "tm"), P()),
        out_specs=(P("groups", None, "tm"), P("groups", None)),
        check_vma=False,
    )
```

```python
import functools

import jax
import jax.numpy as jnp
from jax import lax
from jax.experimental import pallas as pl
from jax.experimental.pallas import tpu as pltpu
from jax.sharding import PartitionSpec as P

ETA_CODE = 2.0
LAM = 0.1
ETA_FILT = 0.5
EPS = 1e-06

F32 = jnp.float32
BF16 = jnp.bfloat16
HOP = BF16
LANES = 128
GROUP = 8
CHUNKS = 3
PACK = 16
PITCH = 17
VMEM_BYTES = 5 << 20


def chunk_starts(chans):
    return [0, chans // 4, chans // 2, chans]


def fetch_parts(source, target, arrived, starts):
    copies = {}
    for step, first in enumerate(starts[:-1]):
        rows = pl.ds(first, starts[step + 1] - first)
        copies[first] = pltpu.make_async_copy(source.at[rows], target.at[rows], arrived.at[step])
        copies[first].start()
    return copies


def lane_index(shape):
    return lax.broadcasted_iota(jnp.int32, shape, 1)


def parity():
    return lax.rem(lax.axis_index("tm"), 2)


def in_vmem():
    return pl.BlockSpec(memory_space=pltpu.VMEM)


def in_hbm():
    return pl.BlockSpec(memory_space=pltpu.HBM)


def spread_kernel(codes_hbm, signal_hbm, filters_hbm, codes_ref, filters_ref, far_ref, far_sent_ref, near_ref, signal_ref, shear_ref, arrived, small):
    chans, count, local_len = codes_ref.shape
    taps = filters_ref.shape[1]
    filters_in = pltpu.make_async_copy(filters_hbm, filters_ref, small.at[0])
    signal_in = pltpu.make_async_copy(signal_hbm, signal_ref, small.at[1])
    filters_in.start()
    fetches = fetch_parts(codes_hbm, codes_ref, arrived, chunk_starts(chans))
    signal_in.start()
    filters_in.wait()
    dict_t = filters_ref[...].T.astype(BF16)
    early, late = dict_t[:LANES], dict_t[LANES:]
    none = jnp.zeros((LANES, count), BF16)
    dict_rows = jnp.concatenate(
        [
            jnp.concatenate([early, none], axis=1),
            jnp.concatenate([late, early], axis=1),
            jnp.concatenate([none, late], axis=1),
        ],
        axis=0,
    )
    lane = lane_index((PACK, LANES))
    zero = jnp.zeros((PACK, LANES), BF16)
    even = parity() == 0

    def finish(first):
        total = jnp.zeros((PACK, 4 * LANES), F32)
        for r in range(PACK):
            parts = [shear_ref[n, pl.ds(PITCH * first + r, PACK, stride=PITCH), :] for n in range(4)]
            row = jnp.concatenate(parts, axis=1)
            total += pltpu.roll(row, r, 1) if r else row
        rows = slice(first, first + PACK)
        own = total[:, :taps] - signal_ref[rows, :].astype(F32)
        onward = total[:, taps:]
        near_ref[rows, :] = jnp.where(even, onward, own)
        far = jnp.where(even, own, onward)
        far_ref[rows, :] = far
        far_sent_ref[rows, :] = far.astype(far_sent_ref.dtype)

    for first in range(0, chans, PACK):
        if first == PACK:
            signal_in.wait()
        for c in range(first, first + PACK, 2):
            if c in fetches:
                fetches[c].wait()
            pair = [codes_ref[c], codes_ref[c + 1]]
            halves = [jnp.concatenate([x[:, n * LANES : (n + 1) * LANES] for x in pair], axis=1) for n in range(2)]
            terms = jnp.dot(dict_rows, jnp.concatenate(halves, axis=0), preferred_element_type=F32).astype(BF16)
            for j in range(2):
                sums = [None] * 4
                for m in range(LANES // PACK):
                    diagonals = [
                        terms[n * LANES + PACK * m : n * LANES + PACK * (m + 1), j * LANES : (j + 1) * LANES]
                        for n in range(3)
                    ]
                    if m == 0:
                        sums = [d.astype(F32) for d in diagonals] + [jnp.zeros((PACK, LANES), F32)]
                        continue
                    turned = [pltpu.roll(d, PACK * m, 1) for d in diagonals]
                    inside = lane >= PACK * m
                    sums[0] += jnp.where(inside, turned[0], zero).astype(F32)
                    sums[1] += jnp.where(inside, turned[1], turned[0]).astype(F32)
                    sums[2] += jnp.where(inside, turned[2], turned[1]).astype(F32)
                    sums[3] += jnp.where(inside, zero, turned[2]).astype(F32)
                for n in range(4):
                    shear_ref[n, PITCH * (c + j) : PITCH * (c + j) + PACK, :] = sums[n]
        if first:
            finish(first - PACK)
    finish(chans - PACK)


def hankel_block(shifted, lane):
    parts = [[], [], []]
    for m in range(LANES // PACK):
        for n in range(3):
            low = shifted[:, n * LANES : (n + 1) * LANES]
            if m:
                high = shifted[:, (n + 1) * LANES : (n + 2) * LANES]
                low = pltpu.roll(jnp.where(lane >= PACK * m, low, high), LANES - PACK * m, 1)
            parts[n].append(low)
    first, second, third = (jnp.concatenate(p, axis=0) for p in parts)
    top = jnp.concatenate([first, second], axis=1)
    bottom = jnp.concatenate([second, third], axis=1)
    return jnp.concatenate([top, bottom], axis=0)


def dict_kernel(codes_ref, sent_near_ref, sent_far_ref, got_near_ref, got_far_ref, mine_ref, other_ref, shifted_ref, wide_ref):
    chans, count, local_len = codes_ref.shape
    me = lax.axis_index("tm")
    even = lax.rem(me, 2) == 0
    last = me == lax.axis_size("tm") - 1
    own = jnp.where(even, sent_far_ref[...], sent_near_ref[...])
    onward = jnp.where(even, sent_near_ref[...], sent_far_ref[...])
    got_far = got_far_ref[...].astype(F32)
    before = jnp.where(even, got_far, got_near_ref[...])
    after = jnp.where(even, got_near_ref[...], got_far)
    following = jnp.where(last, 0.0, onward + after)
    error = jnp.concatenate([own + before, following], axis=1).astype(BF16)
    width = error.shape[1]
    lane = lane_index((PACK, LANES))
    total = jnp.zeros((count, width // 2), F32)
    for first in range(0, chans, PACK):
        rows = error[first : first + PACK]
        for r in range(PACK):
            moved = (pltpu.roll(rows, width - r, 1) if r else rows).astype(F32)
            for n in range(4):
                wide_ref[n, pl.ds(first * PITCH + r, PACK, stride=PITCH), :] = moved[:, n * LANES : (n + 1) * LANES]
        for c in range(first, first + PACK):
            rows_c = pl.ds(c * PITCH, PACK)
            shifted = jnp.concatenate([wide_ref[n, rows_c, :] for n in range(4)], axis=1).astype(BF16)
            shifted_ref[c] = shifted
            total += jnp.dot(codes_ref[c], hankel_block(shifted, lane), preferred_element_type=F32)
    half = count // 2
    mine_ref[...] = jnp.where(even, total[:half], total[half:])
    other_ref[...] = jnp.where(even, total[half:], total[:half])


def codes_kernel(first, sum_ref, codes_ref, shifted_ref, filters_ref, *refs):
    new_hbm, kept_ref, new_ref, left = refs[-4:]
    kept_ref[...] = sum_ref[...]
    chans = new_ref.shape[0]
    dict_b = filters_ref[...].astype(BF16)
    lane = lane_index((PACK, LANES))
    stores = []
    done = 0
    for c in range(chans):
        grad = jnp.dot(dict_b, hankel_block(shifted_ref[first + c], lane), preferred_element_type=F32)
        moved = codes_ref[first + c].astype(F32) - ETA_CODE * grad
        new_ref[c] = (moved - jnp.clip(moved, -LAM, LAM)).astype(BF16)
        if c + 1 == chans or (c + 1) % GROUP == 0:
            rows = pl.ds(done, c + 1 - done)
            target = new_hbm.at[pl.ds(first + done, c + 1 - done)]
            stores.append(pltpu.make_async_copy(new_ref.at[rows], target, left.at[len(stores)]))
            stores[-1].start()
            done = c + 1
    for store in stores:
        store.wait()


def step_codes(first, chans, total, codes, shifted, filters, partial):
    count, local_len = codes.shape[1:]
    earlier = [] if partial is None else [pltpu.with_memory_space_constraint(partial, pltpu.HBM)]
    return pl.pallas_call(
        functools.partial(codes_kernel, first),
        in_specs=[in_vmem()] * 4 + [in_hbm() for _ in earlier],
        out_specs=[in_hbm(), in_vmem()],
        out_shape=[
            pltpu.HBM(codes.shape, BF16),
            jax.ShapeDtypeStruct(total.shape, total.dtype),
        ],
        scratch_shapes=[
            pltpu.VMEM((chans, count, local_len), BF16),
            pltpu.SemaphoreType.DMA((-(-chans // GROUP),)),
        ],
        input_output_aliases={4: 0} if earlier else {},
        compiler_params=pltpu.CompilerParams(vmem_limit_bytes=VMEM_BYTES),
        cost_estimate=pl.CostEstimate(
            flops=2 * chans * count * local_len * shifted.shape[2] // 2,
            bytes_accessed=4 * chans * count * local_len,
            transcendentals=0,
        ),
        name="codes_step",
    )(total, codes, shifted, filters, *earlier)


def normalize_kernel(scale, total_ref, last_ref, filters_ref, out_ref):
    half = out_ref.shape[0]
    rows = pl.ds(pl.multiple_of(parity() * half, 8), half)
    total = total_ref[...].astype(F32) + last_ref[...].astype(F32)
    stepped = filters_ref[rows, :] - ETA_FILT * (total / scale)
    out_ref[...] = stepped / jnp.sqrt(jnp.sum(stepped * stepped, axis=1, keepdims=True) + EPS)


def join_kernel(mine_ref, other_ref, out_ref):
    half = mine_ref.shape[0]
    even = parity() == 0
    out_ref[:half, :] = jnp.where(even, mine_ref[...], other_ref[...])
    out_ref[half:, :] = jnp.where(even, other_ref[...], mine_ref[...])


def exchange_rounds(devices):
    distance, rounds = 2, []
    while distance < devices:
        both = 4 * distance < devices
        rounds.append([distance, 2 * distance, 3 * distance] if both else [distance])
        distance *= 4 if both else 2
    return rounds


def part_ends(chans, rounds):
    weights = [4 if len(distances) > 1 else 3 for distances in rounds]
    return [chans * sum(weights[:n]) // sum(weights) for n in range(len(rounds) + 1)]


def exchange(block, distance):
    size = lax.axis_size("tm")
    return lax.ppermute(block, "tm", [(i, i ^ distance) for i in range(size)])


def shards(signal, codes, filters):
    chans, count, local_len = codes.shape
    taps = filters.shape[1]
    devices = lax.axis_size("tm")
    half = count // 2
    params = pltpu.CompilerParams(vmem_limit_bytes=VMEM_BYTES)
    halo = jax.ShapeDtypeStruct((chans, taps), F32)
    matmul_flops = 2 * chans * count * local_len * taps
    held, held_filters, far, sent_far, sent_near = pl.pallas_call(
        spread_kernel,
        in_specs=[in_hbm()] * 3,
        out_specs=[in_vmem()] * 5,
        out_shape=[
            jax.ShapeDtypeStruct(codes.shape, BF16),
            jax.ShapeDtypeStruct(filters.shape, F32),
            halo,
            jax.ShapeDtypeStruct(halo.shape, HOP),
            halo,
        ],
        scratch_shapes=[
            pltpu.VMEM(signal.shape, BF16),
            pltpu.VMEM((4, PITCH * (chans + 1), LANES), F32),
            pltpu.SemaphoreType.DMA((CHUNKS,)),
            pltpu.SemaphoreType.DMA((2,)),
        ],
        compiler_params=params,
        cost_estimate=pl.CostEstimate(flops=matmul_flops, bytes_accessed=codes.size * 2, transcendentals=0),
        name="spread",
    )(*(pltpu.with_memory_space_constraint(a, pltpu.HBM) for a in (codes, signal, filters)))

    across = [(i, i + 1) for i in range(1, devices - 1, 2)]
    across += [(j, i) for i, j in across]
    got_far = lax.ppermute(sent_far, "tm", across)
    got_near = exchange(sent_near, 1)

    mine, other, shifted = pl.pallas_call(
        dict_kernel,
        in_specs=[in_vmem()] * 5,
        out_specs=[in_vmem()] * 3,
        out_shape=[
            jax.ShapeDtypeStruct((half, taps), F32),
            jax.ShapeDtypeStruct((half, taps), F32),
            jax.ShapeDtypeStruct((chans, PACK, 2 * taps), BF16),
        ],
        scratch_shapes=[pltpu.VMEM((4, PITCH * (chans + 1), LANES), F32)],
        compiler_params=params,
        cost_estimate=pl.CostEstimate(flops=matmul_flops, bytes_accessed=codes.size * 2, transcendentals=0),
        name="dict_grad",
    )(held, sent_near, far, got_near, got_far)

    total = mine + exchange(other, 1)
    rounds = exchange_rounds(devices)
    ends = part_ends(chans, rounds)
    new_codes = None
    for place, distances in enumerate(rounds):
        sent = total.astype(HOP)
        received = [exchange(sent, d) for d in distances]
        first, end = ends[place], ends[place + 1]
        new_codes, kept = step_codes(first, end - first, sent, held, shifted, held_filters, new_codes)
        if place + 1 < len(rounds):
            total = kept.astype(F32) + received[0].astype(F32)
            if len(received) > 1:
                total += received[1].astype(F32) + received[2].astype(F32)
    mine = pl.pallas_call(
        functools.partial(normalize_kernel, float(chans * local_len * devices)),
        in_specs=[in_vmem()] * 3,
        out_specs=in_vmem(),
        out_shape=jax.ShapeDtypeStruct((half, taps), F32),
        compiler_params=params,
        name="normalize",
    )(kept, received[0], held_filters)
    new_filters = pl.pallas_call(
        join_kernel,
        in_specs=[in_vmem()] * 2,
        out_specs=in_vmem(),
        out_shape=jax.ShapeDtypeStruct((count, taps), F32),
        compiler_params=params,
        name="join",
    )(mine, exchange(mine, 1))
    return (new_codes, new_filters)


def solution(mesh):
    return jax.shard_map(
        shards,
        mesh=mesh,
        in_specs=(P("groups", "tm"), P("groups", None, "tm"), P()),
        out_specs=(P("groups", None, "tm"), P("groups", None)),
        check_vma=False,
    )
```

```python
import functools

import jax
import jax.numpy as jnp
from jax import lax
from jax.experimental import pallas as pl
from jax.experimental.pallas import tpu as pltpu
from jax.sharding import PartitionSpec as P

ETA_CODE = 2.0
LAM = 0.1
ETA_FILT = 0.5
EPS = 1e-06

F32 = jnp.float32
BF16 = jnp.bfloat16
HOP = BF16
LANES = 128
GROUP = 8
CHUNKS = 3
PACK = 16
PITCH = 17
SUMS = 8
SUM_PITCH = 9
VMEM_BYTES = 5 << 20


def chunk_starts(chans):
    return [0, chans // 4, chans // 2, chans]


def fetch_parts(source, target, arrived, starts):
    copies = {}
    for step, first in enumerate(starts[:-1]):
        rows = pl.ds(first, starts[step + 1] - first)
        copies[first] = pltpu.make_async_copy(source.at[rows], target.at[rows], arrived.at[step])
        copies[first].start()
    return copies


def lane_index(shape):
    return lax.broadcasted_iota(jnp.int32, shape, 1)


def parity():
    return lax.rem(lax.axis_index("tm"), 2)


def in_vmem():
    return pl.BlockSpec(memory_space=pltpu.VMEM)


def in_hbm():
    return pl.BlockSpec(memory_space=pltpu.HBM)


def spread_kernel(codes_hbm, signal_hbm, filters_hbm, codes_ref, filters_ref, far_ref, far_sent_ref, near_ref, signal_ref, shear_ref, arrived, small):
    chans, count, local_len = codes_ref.shape
    taps = filters_ref.shape[1]
    filters_in = pltpu.make_async_copy(filters_hbm, filters_ref, small.at[0])
    signal_in = pltpu.make_async_copy(signal_hbm, signal_ref, small.at[1])
    filters_in.start()
    fetches = fetch_parts(codes_hbm, codes_ref, arrived, chunk_starts(chans))
    signal_in.start()
    filters_in.wait()
    dict_t = filters_ref[...].T.astype(BF16)
    early, late = dict_t[:LANES], dict_t[LANES:]
    none = jnp.zeros((LANES, count), BF16)
    dict_rows = jnp.concatenate(
        [
            jnp.concatenate([early, none], axis=1),
            jnp.concatenate([late, early], axis=1),
            jnp.concatenate([none, late], axis=1),
        ],
        axis=0,
    )
    lane = lane_index((PACK, LANES))
    zero = jnp.zeros((PACK, LANES), BF16)
    even = parity() == 0

    def finish(first):
        total = jnp.zeros((PACK, 4 * LANES), F32)
        for r in range(SUMS):
            parts = [shear_ref[n, pl.ds(SUM_PITCH * first + r, PACK, stride=SUM_PITCH), :] for n in range(4)]
            row = jnp.concatenate(parts, axis=1)
            total += pltpu.roll(row, r, 1) if r else row
        rows = slice(first, first + PACK)
        own = total[:, :taps] - signal_ref[rows, :].astype(F32)
        onward = total[:, taps:]
        near_ref[rows, :] = jnp.where(even, onward, own)
        far = jnp.where(even, own, onward)
        far_ref[rows, :] = far
        far_sent_ref[rows, :] = far.astype(far_sent_ref.dtype)

    for first in range(0, chans, PACK):
        if first == PACK:
            signal_in.wait()
        for c in range(first, first + PACK, 2):
            if c in fetches:
                fetches[c].wait()
            pair = [codes_ref[c], codes_ref[c + 1]]
            halves = [jnp.concatenate([x[:, n * LANES : (n + 1) * LANES] for x in pair], axis=1) for n in range(2)]
            terms = jnp.dot(dict_rows, jnp.concatenate(halves, axis=0), preferred_element_type=F32)
            sums = [None] * 4
            for m in range(LANES // SUMS):
                diagonals = []
                for n in range(3):
                    rows = terms[n * LANES + SUMS * m : n * LANES + SUMS * (m + 1)]
                    diagonals.append(jnp.concatenate([rows[:, :LANES], rows[:, LANES:]], axis=0))
                if m == 0:
                    sums = diagonals + [jnp.zeros((2 * SUMS, LANES), F32)]
                    continue
                turned = [pltpu.roll(d.astype(BF16), SUMS * m, 1) for d in diagonals]
                inside = lane >= SUMS * m
                sums[0] += jnp.where(inside, turned[0], zero).astype(F32)
                sums[1] += jnp.where(inside, turned[1], turned[0]).astype(F32)
                sums[2] += jnp.where(inside, turned[2], turned[1]).astype(F32)
                sums[3] += jnp.where(inside, zero, turned[2]).astype(F32)
            for j in range(2):
                for n in range(4):
                    place = SUM_PITCH * (c + j)
                    shear_ref[n, place : place + SUMS, :] = sums[n][SUMS * j : SUMS * (j + 1)]
        if first:
            finish(first - PACK)
    finish(chans - PACK)


def hankel_block(shifted, lane):
    parts = [[], [], []]
    for m in range(LANES // PACK):
        for n in range(3):
            low = shifted[:, n * LANES : (n + 1) * LANES]
            if m:
                high = shifted[:, (n + 1) * LANES : (n + 2) * LANES]
                low = pltpu.roll(jnp.where(lane >= PACK * m, low, high), LANES - PACK * m, 1)
            parts[n].append(low)
    first, second, third = (jnp.concatenate(p, axis=0) for p in parts)
    top = jnp.concatenate([first, second], axis=1)
    bottom = jnp.concatenate([second, third], axis=1)
    return jnp.concatenate([top, bottom], axis=0)


def dict_kernel(codes_ref, sent_near_ref, sent_far_ref, got_near_ref, got_far_ref, mine_ref, other_ref, shifted_ref, wide_ref):
    chans, count, local_len = codes_ref.shape
    me = lax.axis_index("tm")
    even = lax.rem(me, 2) == 0
    last = me == lax.axis_size("tm") - 1
    own = jnp.where(even, sent_far_ref[...], sent_near_ref[...])
    onward = jnp.where(even, sent_near_ref[...], sent_far_ref[...])
    got_far = got_far_ref[...].astype(F32)
    before = jnp.where(even, got_far, got_near_ref[...])
    after = jnp.where(even, got_near_ref[...], got_far)
    following = jnp.where(last, 0.0, onward + after)
    error = jnp.concatenate([own + before, following], axis=1).astype(BF16)
    width = error.shape[1]
    lane = lane_index((PACK, LANES))
    total = jnp.zeros((count, width // 2), F32)
    for first in range(0, chans, PACK):
        rows = error[first : first + PACK]
        for r in range(PACK):
            moved = (pltpu.roll(rows, width - r, 1) if r else rows).astype(F32)
            for n in range(4):
                wide_ref[n, pl.ds(first * PITCH + r, PACK, stride=PITCH), :] = moved[:, n * LANES : (n + 1) * LANES]
        for c in range(first, first + PACK):
            rows_c = pl.ds(c * PITCH, PACK)
            shifted = jnp.concatenate([wide_ref[n, rows_c, :] for n in range(4)], axis=1).astype(BF16)
            shifted_ref[c] = shifted
            total += jnp.dot(codes_ref[c], hankel_block(shifted, lane), preferred_element_type=F32)
    half = count // 2
    mine_ref[...] = jnp.where(even, total[:half], total[half:])
    other_ref[...] = jnp.where(even, total[half:], total[:half])


def codes_kernel(first, sum_ref, codes_ref, shifted_ref, filters_ref, *refs):
    new_hbm, kept_ref, new_ref, left = refs[-4:]
    kept_ref[...] = sum_ref[...]
    chans = new_ref.shape[0]
    dict_b = filters_ref[...].astype(BF16)
    lane = lane_index((PACK, LANES))
    stores = []
    done = 0
    for c in range(chans):
        grad = jnp.dot(dict_b, hankel_block(shifted_ref[first + c], lane), preferred_element_type=F32)
        moved = codes_ref[first + c].astype(F32) - ETA_CODE * grad
        new_ref[c] = (moved - jnp.clip(moved, -LAM, LAM)).astype(BF16)
        if c + 1 == chans or (c + 1) % GROUP == 0:
            rows = pl.ds(done, c + 1 - done)
            target = new_hbm.at[pl.ds(first + done, c + 1 - done)]
            stores.append(pltpu.make_async_copy(new_ref.at[rows], target, left.at[len(stores)]))
            stores[-1].start()
            done = c + 1
    for store in stores:
        store.wait()


def step_codes(first, chans, total, codes, shifted, filters, partial):
    count, local_len = codes.shape[1:]
    earlier = [] if partial is None else [pltpu.with_memory_space_constraint(partial, pltpu.HBM)]
    return pl.pallas_call(
        functools.partial(codes_kernel, first),
        in_specs=[in_vmem()] * 4 + [in_hbm() for _ in earlier],
        out_specs=[in_hbm(), in_vmem()],
        out_shape=[
            pltpu.HBM(codes.shape, BF16),
            jax.ShapeDtypeStruct(total.shape, total.dtype),
        ],
        scratch_shapes=[
            pltpu.VMEM((chans, count, local_len), BF16),
            pltpu.SemaphoreType.DMA((-(-chans // GROUP),)),
        ],
        input_output_aliases={4: 0} if earlier else {},
        compiler_params=pltpu.CompilerParams(vmem_limit_bytes=VMEM_BYTES),
        cost_estimate=pl.CostEstimate(
            flops=2 * chans * count * local_len * shifted.shape[2] // 2,
            bytes_accessed=4 * chans * count * local_len,
            transcendentals=0,
        ),
        name="codes_step",
    )(total, codes, shifted, filters, *earlier)


def normalize_kernel(scale, total_ref, last_ref, filters_ref, out_ref):
    half = out_ref.shape[0]
    rows = pl.ds(pl.multiple_of(parity() * half, 8), half)
    total = total_ref[...].astype(F32) + last_ref[...].astype(F32)
    stepped = filters_ref[rows, :] - ETA_FILT * (total / scale)
    out_ref[...] = stepped / jnp.sqrt(jnp.sum(stepped * stepped, axis=1, keepdims=True) + EPS)


def join_kernel(mine_ref, other_ref, out_ref):
    half = mine_ref.shape[0]
    even = parity() == 0
    out_ref[:half, :] = jnp.where(even, mine_ref[...], other_ref[...])
    out_ref[half:, :] = jnp.where(even, other_ref[...], mine_ref[...])


def exchange_rounds(devices):
    distance, rounds = 2, []
    while distance < devices:
        both = 4 * distance < devices
        rounds.append([distance, 2 * distance, 3 * distance] if both else [distance])
        distance *= 4 if both else 2
    return rounds


def part_ends(chans, rounds):
    weights = [4 if len(distances) > 1 else 3 for distances in rounds]
    return [chans * sum(weights[:n]) // sum(weights) for n in range(len(rounds) + 1)]


def exchange(block, distance):
    size = lax.axis_size("tm")
    return lax.ppermute(block, "tm", [(i, i ^ distance) for i in range(size)])


def shards(signal, codes, filters):
    chans, count, local_len = codes.shape
    taps = filters.shape[1]
    devices = lax.axis_size("tm")
    half = count // 2
    params = pltpu.CompilerParams(vmem_limit_bytes=VMEM_BYTES)
    halo = jax.ShapeDtypeStruct((chans, taps), F32)
    matmul_flops = 2 * chans * count * local_len * taps
    held, held_filters, far, sent_far, sent_near = pl.pallas_call(
        spread_kernel,
        in_specs=[in_hbm()] * 3,
        out_specs=[in_vmem()] * 5,
        out_shape=[
            jax.ShapeDtypeStruct(codes.shape, BF16),
            jax.ShapeDtypeStruct(filters.shape, F32),
            halo,
            jax.ShapeDtypeStruct(halo.shape, HOP),
            halo,
        ],
        scratch_shapes=[
            pltpu.VMEM(signal.shape, BF16),
            pltpu.VMEM((4, SUM_PITCH * (chans + 1), LANES), F32),
            pltpu.SemaphoreType.DMA((CHUNKS,)),
            pltpu.SemaphoreType.DMA((2,)),
        ],
        compiler_params=params,
        cost_estimate=pl.CostEstimate(flops=matmul_flops, bytes_accessed=codes.size * 2, transcendentals=0),
        name="spread",
    )(*(pltpu.with_memory_space_constraint(a, pltpu.HBM) for a in (codes, signal, filters)))

    across = [(i, i + 1) for i in range(1, devices - 1, 2)]
    across += [(j, i) for i, j in across]
    got_far = lax.ppermute(sent_far, "tm", across)
    got_near = exchange(sent_near, 1)

    mine, other, shifted = pl.pallas_call(
        dict_kernel,
        in_specs=[in_vmem()] * 5,
        out_specs=[in_vmem()] * 3,
        out_shape=[
            jax.ShapeDtypeStruct((half, taps), F32),
            jax.ShapeDtypeStruct((half, taps), F32),
            jax.ShapeDtypeStruct((chans, PACK, 2 * taps), BF16),
        ],
        scratch_shapes=[pltpu.VMEM((4, PITCH * (chans + 1), LANES), F32)],
        compiler_params=params,
        cost_estimate=pl.CostEstimate(flops=matmul_flops, bytes_accessed=codes.size * 2, transcendentals=0),
        name="dict_grad",
    )(held, sent_near, far, got_near, got_far)

    total = mine + exchange(other, 1)
    rounds = exchange_rounds(devices)
    ends = part_ends(chans, rounds)
    new_codes = None
    for place, distances in enumerate(rounds):
        sent = total.astype(HOP)
        received = [exchange(sent, d) for d in distances]
        first, end = ends[place], ends[place + 1]
        new_codes, kept = step_codes(first, end - first, sent, held, shifted, held_filters, new_codes)
        if place + 1 < len(rounds):
            total = kept.astype(F32) + received[0].astype(F32)
            if len(received) > 1:
                total += received[1].astype(F32) + received[2].astype(F32)
    mine = pl.pallas_call(
        functools.partial(normalize_kernel, float(chans * local_len * devices)),
        in_specs=[in_vmem()] * 3,
        out_specs=in_vmem(),
        out_shape=jax.ShapeDtypeStruct((half, taps), F32),
        compiler_params=params,
        name="normalize",
    )(kept, received[0], held_filters)
    new_filters = pl.pallas_call(
        join_kernel,
        in_specs=[in_vmem()] * 2,
        out_specs=in_vmem(),
        out_shape=jax.ShapeDtypeStruct((count, taps), F32),
        compiler_params=params,
        name="join",
    )(mine, exchange(mine, 1))
    return (new_codes, new_filters)


def solution(mesh):
    return jax.shard_map(
        shards,
        mesh=mesh,
        in_specs=(P("groups", "tm"), P("groups", None, "tm"), P()),
        out_specs=(P("groups", None, "tm"), P("groups", None)),
        check_vma=False,
    )
```
